32 devices in a mesh: group: 2 (over y), pool: 4 (over x, core), tensor: 4 (over z).
Axes of the slice: x: 2, y: 2, z: 4, core: 2. Of those that a mesh axis runs over, the one named last changes fastest.
Arguments:
- tokens: bfloat16 [8192, 8192], P(('group', 'pool'), 'tensor'), parts along dimension 0, may hold values from -6 to 6
- base_projection_weight: bfloat16 [8192, 2048], P('tensor'), may hold values from -0.09375 to 0.09375
- adapter_down_weight: bfloat16 [64, 8192, 128], P(('group', 'pool'), 'tensor'), parts along dimension 0, may hold values from -0.0625 to 0.0625
- adapter_up_weight: bfloat16 [64, 64, 2048], P(('group', 'pool'), None, 'tensor'), parts along dimension 0, may hold values from -0.75 to 0.75
- batch_adapter_ids: int32 [8, 8], P(('group', 'pool')), parts along dimension 0, may hold values from 0 to 31, as said below
- batch_request_counts: int32 [8, 8], P(('group', 'pool')), parts along dimension 0, may hold values from 1 to 32, 128 in all within a row
- adapter_storage_row: int32 [64], P('group'), parts along dimension 0, may hold values from 0 to 31, as said below
Outputs:
- key_value: bfloat16 [8192, 2048], P(('group', 'pool'), 'tensor'), parts along dimension 0
The draws below stay inside these ranges and needn't reach their ends.
There are 2 independent parts, one for each index of `group`. The reference program is written for one: setup_inputs(seed, part) draws one part's arguments, and reference() takes and returns one part's arrays. A program takes and returns all parts, laid end to end along the dimension named above; an argument that names none is the same for every part. Nothing has to cross between parts.
Inputs may be any that keep to these rules, and one draw needn't show every extreme that they name: `batch_adapter_ids`: within one row (one pool index's batches) the ids are distinct, and exactly 2 of them have adapter_storage_row // 8 equal to each value. A permutation: adapter a lies at row adapter_storage_row[a] of adapter_down_weight and adapter_up_weight, on pool index adapter_storage_row[a] // 8. `batch_request_counts`: each row sums to 128; its largest entry is exactly 32.
All inputs are finite; a program needn't handle non-finite values.
Results may differ from the reference program's by a relative error of at most 0.013.
Values may be sent and summed in bfloat16 or wider, within the bound.
A program may use at most 128 MiB of HBM per device.

```python
import math
import jax
import jax.numpy as jnp
import numpy as np
from jax import lax

MODEL_WIDTH = 8192
KEY_VALUE_WIDTH = 1024
ADAPTER_RANK = 64
DRAFT = 8
REQ_DEV = 128
SLOTS_DEV = 8
CAP = 2
POOL_OWNERS = 4
USED = 8
MAXREQ = 32
MAXT = 256
TOK_DEV = 1024
TOKEN_COUNT = 4096
ADAPTER_POOL = 32
N_TENSOR = 4


def shared_layout(key):
    home_key, pick_key = jax.random.split(key)
    home_rows = jax.random.permutation(home_key, ADAPTER_POOL).astype(jnp.int32)
    stored_adapter = jnp.argsort(home_rows, stable=True).astype(jnp.int32)
    holder_keys = jax.random.split(pick_key, POOL_OWNERS)

    def one_holder(holder_key):
        slot_key, mix_key = jax.random.split(holder_key, 2)
        slot_keys = jax.random.split(slot_key, POOL_OWNERS)
        slot_choice = jax.vmap(lambda one_key: jax.random.permutation(one_key, SLOTS_DEV))(slot_keys)[:, :CAP]
        storage_index = (jnp.arange(POOL_OWNERS, dtype=jnp.int32)[:, None] * SLOTS_DEV + slot_choice).astype(jnp.int32)
        shuffle = jax.random.permutation(mix_key, POOL_OWNERS * CAP).astype(jnp.int32)
        return stored_adapter[storage_index.reshape(-1)[shuffle]]
    return (home_rows, jax.vmap(one_holder)(holder_keys).astype(jnp.int32))


def draw_batch_adapter_ids(key, part):
    return shared_layout(key)[1]


def draw_adapter_storage_row(key, part):
    return shared_layout(key)[0]


def raised(drawn, key, source, target, blocks, factor):
    def block_of(axis_at):
        return (jnp.arange(drawn.shape[axis_at]) // (drawn.shape[axis_at] // blocks)).reshape((-1,) + (1,) * (drawn.ndim - 1 - axis_at))

    first = jax.random.permutation(key, blocks)[block_of(target)]
    other_side = (block_of(target) + blocks // 2) % blocks
    return jnp.where((block_of(source) == first) | (block_of(source) == other_side), factor * drawn, drawn)


def shard_levels(own_key, shape, cuts, least, top_value):
    factor_of, own = 1.0, jax.random.fold_in(own_key, 6)
    for axis_at, shards_of in cuts:
        heights = jnp.exp(jax.random.uniform(jax.random.fold_in(own, axis_at), (shards_of,), jnp.float32, least / len(cuts), top_value / len(cuts)))
        factor_of = factor_of * jnp.repeat(heights, shape[axis_at] // shards_of).reshape([-1 if axis == axis_at else 1 for axis in range(len(shape))])
    return factor_of


def split_up(count, total, limit, skew):
    loads = [(1 << 20) // math.isqrt(rank ** skew) + 1 for rank in range(2, count + 1)]
    surplus, given = total - limit - (count - 1), [1] * (count - 1)
    while surplus > 0:
        candidates = [i for i in range(count - 1) if given[i] < limit]
        pool, remaining = sum([loads[i] for i in candidates]), surplus
        for i in candidates:
            extra = min(limit - given[i], max(1, remaining * loads[i] // pool), surplus)
            given[i] = given[i] + extra
            surplus = surplus - extra
    return np.array([limit] + given)


def uneven(rng, amount, total, bound, lean):
    if amount == 2:
        one = jax.random.randint(rng, (), max(1, total - bound), min(bound, total - 1) + 1)
        return jnp.stack([one, total - one])
    sizes = jnp.asarray(split_up(amount, total, bound, lean), jnp.int32)
    couples = (amount - 1) // 2
    source_of, receiver = sizes[1:1 + 2 * couples:2], sizes[2:2 + 2 * couples:2]
    room = jnp.minimum(source_of - 1, bound - receiver)
    shifted = jax.random.randint(jax.random.fold_in(rng, 1), (couples,), 0, 1 << 20) % (room + 1)
    sizes = sizes.at[1:1 + 2 * couples:2].set(source_of - shifted).at[2:2 + 2 * couples:2].set(receiver + shifted)
    return sizes[jax.random.permutation(jax.random.fold_in(rng, 2), amount)]


def noise(own_key, dims, scale, limit, cuts=(), kind=jnp.bfloat16):
    gain = shard_levels(own_key, dims, cuts, -0.22, 0.18) if cuts else 1.0
    result = jax.random.normal(own_key, dims, jnp.float32) * scale * gain
    return jnp.minimum(jnp.maximum(result, -limit), limit).astype(kind)


def bell_draw_with(own_key, dims, width, reach, shards, heavy, held_as=jnp.bfloat16):
    result = width * jax.random.normal(own_key, dims, jnp.float32)
    if shards:
        result = result * shard_levels(own_key, dims, shards, -0.22, 0.18)
    return jnp.clip(raised(result, jax.random.fold_in(own_key, 3), *heavy), -reach, reach).astype(held_as)


def setup_inputs(seed: int = 0, part: int = 0) -> dict:
    streams_of = jax.random.split(jax.random.key(seed), 8)
    own_keys = jax.random.split(jax.random.fold_in(streams_of[7], part), 8)
    return {
        "tokens": noise(own_keys[0], (TOKEN_COUNT, MODEL_WIDTH), 1.0, 6.0, ((0, 4), (1, 4))),
        "base_projection_weight": bell_draw_with(streams_of[1], (MODEL_WIDTH, 2 * KEY_VALUE_WIDTH), MODEL_WIDTH ** -0.5, 0.09375, ((0, 4),), (0, 1, 4, 2.0)),
        "adapter_down_weight": noise(own_keys[2], (ADAPTER_POOL, MODEL_WIDTH, 2 * ADAPTER_RANK), MODEL_WIDTH ** -0.5, 0.0625, ((0, 4), (1, 4))),
        "adapter_up_weight": noise(own_keys[3], (ADAPTER_POOL, ADAPTER_RANK, 2 * KEY_VALUE_WIDTH), ADAPTER_RANK ** -0.5, 0.75, ((0, 4), (2, 4))),
        "batch_adapter_ids": draw_batch_adapter_ids(jax.random.fold_in(jax.random.fold_in(streams_of[7], part), 71), part),
        "batch_request_counts": jax.vmap(lambda own: uneven(own, USED, REQ_DEV, MAXREQ, 2))(jax.random.split(own_keys[5], POOL_OWNERS)).reshape((POOL_OWNERS, USED)).astype(jnp.int32),
        "adapter_storage_row": draw_adapter_storage_row(jax.random.fold_in(jax.random.fold_in(streams_of[7], part), 71), part),
    }


def reference(tokens, base_projection_weight, adapter_down_weight, adapter_up_weight, batch_adapter_ids, batch_request_counts, adapter_storage_row):
    width_part = MODEL_WIDTH // N_TENSOR
    feature_blocks = tokens.reshape(TOKEN_COUNT, N_TENSOR, width_part)
    weight_blocks = base_projection_weight.reshape(N_TENSOR, width_part, 2 * KEY_VALUE_WIDTH)

    def add_block(running_totals, block_number):
        features = lax.dynamic_index_in_dim(feature_blocks, block_number, 1, keepdims=False)
        weights = lax.dynamic_index_in_dim(weight_blocks, block_number, 0, keepdims=False)
        partial_sum = jnp.dot(features, weights, preferred_element_type=jnp.float32)
        rounded = lax.optimization_barrier(partial_sum.astype(jnp.bfloat16))
        return running_totals + rounded.astype(jnp.float32), None

    base_accumulator, _ = lax.scan(add_block, jnp.zeros((TOKEN_COUNT, 2 * KEY_VALUE_WIDTH), jnp.float32),
                           jnp.arange(N_TENSOR, dtype=jnp.int32))

    def owner_adapter(pool_owner):
        own_tokens = lax.dynamic_slice_in_dim(tokens, (pool_owner * TOK_DEV).astype(jnp.int32), TOK_DEV, 0)
        padded = jnp.concatenate([own_tokens, jnp.zeros((MAXT, MODEL_WIDTH), tokens.dtype)], 0)
        counts = batch_request_counts[pool_owner]
        starts = ((jnp.cumsum(counts) - counts) * DRAFT).astype(jnp.int32)
        lengths = (counts * DRAFT).astype(jnp.int32)
        storage_index = adapter_storage_row[batch_adapter_ids[pool_owner]]

        def batch_step(batch_position, running_totals):
            starting_row = starts[batch_position]
            segment = lax.dynamic_slice_in_dim(padded, starting_row, MAXT, 0)
            down_weight_block = adapter_down_weight[storage_index[batch_position]]
            up_weight_block = adapter_up_weight[storage_index[batch_position]]
            shrink = jnp.dot(segment, down_weight_block, preferred_element_type=jnp.float32).astype(jnp.bfloat16)
            key_output = jnp.dot(shrink[:, :ADAPTER_RANK], up_weight_block[:, :KEY_VALUE_WIDTH], preferred_element_type=jnp.float32)
            value_output = jnp.dot(shrink[:, ADAPTER_RANK:], up_weight_block[:, KEY_VALUE_WIDTH:], preferred_element_type=jnp.float32)
            adapter_rows = jnp.concatenate([key_output, value_output], 1)
            within_batch = (jnp.arange(MAXT) < lengths[batch_position])[:, None]
            prior_count = lax.dynamic_slice_in_dim(running_totals, starting_row, MAXT, 0)
            return lax.dynamic_update_slice_in_dim(running_totals, prior_count + jnp.where(within_batch, adapter_rows, 0.0), starting_row, 0)

        running_totals = lax.fori_loop(0, USED, batch_step, jnp.zeros((TOK_DEV + MAXT, 2 * KEY_VALUE_WIDTH), jnp.float32))
        return running_totals[:TOK_DEV]

    adapter_accumulator = lax.map(owner_adapter, jnp.arange(POOL_OWNERS, dtype=jnp.int32)).reshape(TOKEN_COUNT, 2 * KEY_VALUE_WIDTH)
    return (base_accumulator + adapter_accumulator).astype(jnp.bfloat16)
```

```python
import functools

import jax
import jax.numpy as jnp
from jax import lax
from jax.experimental import pallas as pl
from jax.experimental.pallas import tpu as pltpu
from jax.sharding import PartitionSpec as P

DRAFT = 8
CAP = 2
SUBS = 4
HELD = 2
MESH = pl.DeviceIdType.MESH
F32 = jnp.float32
BF16 = jnp.bfloat16


def kernel(
    nz,
    npool,
    tok_hbm,
    w_hbm,
    down_hbm,
    up_hbm,
    ids,
    counts,
    row_table,
    out_hbm,
    tok,
    w,
    down,
    up,
    part,
    right_in,
    left_in,
    down_send,
    down_got,
    up_send,
    up_got,
    shrink,
    shr_right,
    shr_left,
    shr_right_in,
    shr_left_in,
    mixed,
    out_v,
    req_out,
    req_in,
    req_s,
    own_s,
    span_s,
    batch_s,
    tok_sem,
    w_sem,
    down_sem,
    up_sem,
    out_sem,
    part_send,
    right_recv,
    left_recv,
    req_send,
    req_recv,
    req_local,
    down_send_sem,
    down_recv,
    up_send_sem,
    up_recv,
    shr_send_sem,
    shr_right_recv,
    shr_left_recv,
):
    z = lax.axis_index("tensor")
    me = lax.axis_index("pool")
    slots = down_hbm.shape[0]
    batches = ids.shape[1]
    sub = tok.shape[1]
    cw = out_v.shape[2]
    rank2 = down_hbm.shape[2]
    rank = rank2 // 2
    first, last = z == 0, z == nz - 1
    middle = jnp.logical_and(z > 0, z < nz - 1)
    upper = lax.div(2 * z, nz)

    def chunk(i):
        return i + (1 - upper) * (nz - 1 - 2 * i)

    def peer(j):
        return lax.rem(lax.div(me, 2) + lax.div(j, 2), npool // 2) * 2 + lax.rem(me + j, 2)

    def tok_copy(s):
        return pltpu.make_async_copy(tok_hbm.at[pl.ds(s * sub, sub)], tok.at[s], tok_sem.at[s])

    def w_copy(d):
        return pltpu.make_async_copy(
            w_hbm.at[:, pl.ds(pl.multiple_of(d * cw, cw), cw)], w.at[d], w_sem.at[d]
        )

    down_copy = pltpu.make_async_copy(down_hbm, down, down_sem)
    up_copy = pltpu.make_async_copy(up_hbm, up, up_sem)

    def right_copy(d, s):
        return pltpu.make_async_remote_copy(
            src_ref=part.at[d, s],
            dst_ref=right_in.at[d, s],
            send_sem=part_send.at[d, s],
            recv_sem=right_recv.at[d, s],
            device_id={"tensor": z + 1},
            device_id_type=MESH,
        )

    def left_copy(d, s):
        return pltpu.make_async_remote_copy(
            src_ref=part.at[d, s],
            dst_ref=left_in.at[d, s],
            send_sem=part_send.at[d, s],
            recv_sem=left_recv.at[d, s],
            device_id={"tensor": z - 1},
            device_id_type=MESH,
        )

    def shr_right_copy(s):
        return pltpu.make_async_remote_copy(
            src_ref=shr_right.at[s],
            dst_ref=shr_right_in.at[s],
            send_sem=shr_send_sem.at[0, s],
            recv_sem=shr_right_recv.at[s],
            device_id={"tensor": z + 1},
            device_id_type=MESH,
        )

    def shr_left_copy(s):
        return pltpu.make_async_remote_copy(
            src_ref=shr_left.at[s],
            dst_ref=shr_left_in.at[s],
            send_sem=shr_send_sem.at[1, s],
            recv_sem=shr_left_recv.at[s],
            device_id={"tensor": z - 1},
            device_id_type=MESH,
        )

    def pool_copy(src, dst, send, recv, p, landing):
        return pltpu.make_async_remote_copy(
            src_ref=src,
            dst_ref=dst,
            send_sem=send.at[p],
            recv_sem=recv.at[landing],
            device_id={"pool": p},
            device_id_type=MESH,
        )

    def req_copy(p, landing):
        return pool_copy(req_out.at[p], req_in.at[landing], req_send, req_recv, p, landing)

    def down_peer(p, landing):
        return pool_copy(
            down_send.at[p], down_got.at[landing], down_send_sem, down_recv, p, landing
        )

    def up_rows(p):
        return pl.ds(pl.multiple_of(p * rank2, rank2), rank2)

    def up_peer(p, landing):
        return pool_copy(
            up_send.at[p], up_got.at[up_rows(landing)], up_send_sem, up_recv, p, landing
        )

    w_copy(chunk(0)).start()
    for s in range(SUBS):
        tok_copy(s).start()
    down_copy.start()
    up_copy.start()
    for i in range(1, nz):
        w_copy(chunk(i)).start()

    barrier = pltpu.get_barrier_semaphore()

    @pl.when(z > 0)
    def _():
        pl.semaphore_signal(barrier, inc=1, device_id={"tensor": z - 1}, device_id_type=MESH)

    @pl.when(z < nz - 1)
    def _():
        pl.semaphore_signal(barrier, inc=1, device_id={"tensor": z + 1}, device_id_type=MESH)

    for j in range(1, npool):
        p = peer(jnp.int32(j))
        pl.semaphore_signal(barrier, inc=1, device_id={"pool": p}, device_id_type=MESH)

    def read_batch(b, row):
        index = row_table[ids[0, b]]
        batch_s[0, b] = index // slots
        batch_s[1, b] = lax.rem(index, slots)
        batch_s[2, b] = row
        after = row + counts[0, b] * DRAFT
        batch_s[3, b] = after
        return after

    lax.fori_loop(0, batches, read_batch, jnp.int32(0))
    lane8 = lax.broadcasted_iota(jnp.int32, (8, 128), 1)

    def read_holder(p, _):
        def match(b, carry):
            seen, r0, b0, e0, r1, b1, e1 = carry
            hit = batch_s[0, b] == p
            one = jnp.logical_and(hit, seen == 0)
            two = jnp.logical_and(hit, seen == 1)
            local, start, end = batch_s[1, b], batch_s[2, b], batch_s[3, b]
            return (
                seen + jnp.where(hit, 1, 0),
                jnp.where(one, local, r0),
                jnp.where(one, start, b0),
                jnp.where(one, end, e0),
                jnp.where(two, local, r1),
                jnp.where(two, start, b1),
                jnp.where(two, end, e1),
            )

        zero = jnp.int32(0)
        _, r0, b0, e0, r1, b1, e1 = lax.fori_loop(0, batches, match, (zero,) * 7)
        own_s[p, 0] = r0
        own_s[p, 1] = r1
        span_s[p, 0] = b0
        span_s[p, 1] = e0
        span_s[p, 2] = b1
        span_s[p, 3] = e1
        req_out[p] = jnp.where(lane8 == 0, r0, jnp.where(lane8 == 1, r1, 0))
        return 0

    lax.fori_loop(0, npool, read_holder, 0)
    pl.semaphore_wait(
        barrier, npool - 1 + jnp.where(z > 0, 1, 0) + jnp.where(z < nz - 1, 1, 0)
    )

    def each_peer(body):
        def step(j, _):
            body(peer(j))
            return 0

        lax.fori_loop(1, npool, step, 0)

    each_peer(lambda p: req_copy(p, me).start())

    def base_block(d, s):
        part[d, s] = jnp.dot(tok[s], w[d], preferred_element_type=F32).astype(BF16)

    def end_send(d, s):
        @pl.when(first)
        def _():
            right_copy(d, s).start()

        @pl.when(last)
        def _():
            left_copy(d, s).start()

    w_copy(chunk(0)).wait()

    def first_chunk(s, _):
        tok_copy(s).wait()
        base_block(chunk(0), s)
        end_send(chunk(0), s)
        return 0

    lax.fori_loop(0, SUBS, first_chunk, 0)

    down_copy.wait()
    up_copy.wait()
    for c in range(CAP):
        down_got[me, :, c * rank2 : (c + 1) * rank2] = down[own_s[me, c]]
        up_got[pl.ds(pl.multiple_of(me * rank2 + c * rank, rank), rank), :] = up[own_s[me, c]]

    def read_request(p):
        req_copy(p, p).wait_recv()
        local = pltpu.make_async_copy(req_in.at[p], req_s.at[p], req_local.at[p])
        local.start()
        local.wait()

    each_peer(read_request)

    def serve(p):
        for c in range(CAP):
            down_send[p, :, c * rank2 : (c + 1) * rank2] = down[req_s[p, 0, c]]
            up_send[p, c * rank : (c + 1) * rank, :] = up[req_s[p, 0, c]]
        down_peer(p, me).start()
        up_peer(p, me).start()

    each_peer(serve)

    def next_chunk(i, _):
        d = chunk(i)
        w_copy(d).wait()

        def rows(s, _):
            base_block(d, s)

            @pl.when(jnp.logical_or(i < nz - 2, jnp.logical_and(i == nz - 2, s < SUBS - HELD)))
            def _():
                end_send(d, s)

            return 0

        return lax.fori_loop(0, SUBS, rows, 0)

    lax.fori_loop(1, nz, next_chunk, 0)

    shrink[...] = jnp.zeros_like(shrink)
    row_of = lax.broadcasted_iota(jnp.int32, (sub, rank2), 0)

    def down_project(p):
        def rows(s, _):
            both = jnp.dot(tok[s], down_got[p], preferred_element_type=F32)
            at = row_of + s * sub
            kept = shrink[s]
            for c in range(CAP):
                use = jnp.logical_and(at >= span_s[p, 2 * c], at < span_s[p, 2 * c + 1])
                kept = jnp.where(use, both[:, c * rank2 : (c + 1) * rank2], kept)
            shrink[s] = kept
            return 0

        lax.fori_loop(0, SUBS, rows, 0)

    def down_from(j, _):
        p = peer(j)
        down_peer(p, p).wait_recv()
        down_project(p)
        return 0

    down_project(me)
    lax.fori_loop(1, 2, down_from, 0)

    @pl.when(middle)
    def _():
        def forward(i, _):
            def rows(s, _):
                r, l = nz - 1 - i, i

                @pl.when(r > z)
                def _():
                    right_copy(r, s).wait_recv()
                    part[r, s] = (part[r, s].astype(F32) + right_in[r, s].astype(F32)).astype(BF16)
                    right_copy(r, s).start()

                @pl.when(l < z)
                def _():
                    left_copy(l, s).wait_recv()
                    part[l, s] = (part[l, s].astype(F32) + left_in[l, s].astype(F32)).astype(BF16)
                    left_copy(l, s).start()

                return 0

            return lax.fori_loop(0, SUBS, rows, 0)

        lax.fori_loop(0, nz - 1, forward, 0)

    lax.fori_loop(2, npool, down_from, 0)

    def shrink_rows(s, _):
        @pl.when(first)
        def _():
            shr_right[s] = shrink[s].astype(BF16)
            shr_right_copy(s).start()

        @pl.when(middle)
        def _():
            shr_right_copy(s).wait_recv()
            shr_right[s] = (shrink[s] + shr_right_in[s].astype(F32)).astype(BF16)
            shr_right_copy(s).start()
            shr_left_copy(s).wait_recv()
            shr_left[s] = (shrink[s] + shr_left_in[s].astype(F32)).astype(BF16)
            shr_left_copy(s).start()
            shrink[s] = (
                shrink[s] + shr_right_in[s].astype(F32) + shr_left_in[s].astype(F32)
            )

        @pl.when(last)
        def _():
            shr_left[s] = shrink[s].astype(BF16)
            shr_left_copy(s).start()

        return 0

    lax.fori_loop(0, SUBS, shrink_rows, 0)
    for s in range(SUBS - HELD, SUBS):
        end_send(chunk(nz - 2), s)

    each_peer(lambda p: up_peer(p, p).wait_recv())
    lane = lax.broadcasted_iota(jnp.int32, (sub, rank2), 1)

    def finish(s, _):
        @pl.when(first)
        def _():
            shr_left_copy(s).wait_recv()
            shrink[s] = shrink[s] + shr_left_in[s].astype(F32)

        @pl.when(last)
        def _():
            shr_right_copy(s).wait_recv()
            shrink[s] = shrink[s] + shr_right_in[s].astype(F32)

        whole = shrink[s]
        swapped = pltpu.roll(whole, rank, 1)
        half = jnp.where(lane // rank == upper, whole, swapped)
        at = row_of + s * sub
        for p in range(npool):
            begin = jnp.where(lane < rank, span_s[p, 0], span_s[p, 2])
            end = jnp.where(lane < rank, span_s[p, 1], span_s[p, 3])
            use = jnp.logical_and(at >= begin, at < end)
            mixed[:, p * rank2 : (p + 1) * rank2] = jnp.where(use, half, 0.0).astype(BF16)
        out = jnp.dot(mixed[...], up_got[...], preferred_element_type=F32)
        out_v[s] = out + part[z, s].astype(F32)

        @pl.when(z > 0)
        def _():
            right_copy(z, s).wait_recv()
            out_v[s] = out_v[s] + right_in[z, s].astype(F32)

        @pl.when(z < nz - 1)
        def _():
            left_copy(z, s).wait_recv()
            out_v[s] = out_v[s] + left_in[z, s].astype(F32)

        part[z, s] = out_v[s].astype(BF16)
        pltpu.make_async_copy(
            part.at[z, s], out_hbm.at[pl.ds(pl.multiple_of(s * sub, sub), sub)], out_sem.at[s]
        ).start()
        return 0

    lax.fori_loop(0, SUBS, finish, 0)

    def sent(s, _):
        pltpu.make_async_copy(
            part.at[z, s], out_hbm.at[pl.ds(pl.multiple_of(s * sub, sub), sub)], out_sem.at[s]
        ).wait()

        def one(d, _):
            @pl.when(d > z)
            def _():
                right_copy(d, s).wait_send()

            @pl.when(d < z)
            def _():
                left_copy(d, s).wait_send()

            return 0

        lax.fori_loop(0, nz, one, 0)

        @pl.when(z < nz - 1)
        def _():
            shr_right_copy(s).wait_send()

        @pl.when(z > 0)
        def _():
            shr_left_copy(s).wait_send()

        return 0

    lax.fori_loop(0, SUBS, sent, 0)

    def pool_sent(p):
        req_copy(p, me).wait_send()
        down_peer(p, me).wait_send()
        up_peer(p, me).wait_send()

    each_peer(pool_sent)


def body(tokens, base_w, down_w, up_w, ids, counts, row_table):
    nz, npool = lax.axis_size("tensor"), lax.axis_size("pool")
    rows, features = tokens.shape
    slots, _, rank2 = down_w.shape
    rank, cw = up_w.shape[1:]
    batches = ids.shape[1]
    sub = rows // SUBS
    any_spec = pl.BlockSpec(memory_space=pl.ANY)
    smem = pl.BlockSpec(memory_space=pltpu.SMEM)
    dma = pltpu.SemaphoreType.DMA
    vmem = pltpu.VMEM
    return pl.pallas_call(
        functools.partial(kernel, nz, npool),
        out_shape=jax.ShapeDtypeStruct((rows, cw), BF16),
        in_specs=[any_spec] * 4 + [smem] * 3,
        out_specs=any_spec,
        scratch_shapes=[
            vmem((SUBS, sub, features), BF16),
            vmem((nz, features, cw), BF16),
            vmem((slots, features, rank2), BF16),
            vmem((slots, rank, cw), BF16),
            vmem((nz, SUBS, sub, cw), BF16),
            vmem((nz, SUBS, sub, cw), BF16),
            vmem((nz, SUBS, sub, cw), BF16),
            vmem((npool, features, CAP * rank2), BF16),
            vmem((npool, features, CAP * rank2), BF16),
            vmem((npool, CAP * rank, cw), BF16),
            vmem((npool * CAP * rank, cw), BF16),
            vmem((SUBS, sub, rank2), F32),
            vmem((SUBS, sub, rank2), BF16),
            vmem((SUBS, sub, rank2), BF16),
            vmem((SUBS, sub, rank2), BF16),
            vmem((SUBS, sub, rank2), BF16),
            vmem((sub, npool * CAP * rank), BF16),
            vmem((SUBS, sub, cw), F32),
            vmem((npool, 8, 128), jnp.int32),
            vmem((npool, 8, 128), jnp.int32),
            pltpu.SMEM((npool, 8, 128), jnp.int32),
            pltpu.SMEM((npool, CAP), jnp.int32),
            pltpu.SMEM((npool, 2 * CAP), jnp.int32),
            pltpu.SMEM((4, batches), jnp.int32),
            dma((SUBS,)),
            dma((nz,)),
            dma,
            dma,
            dma((SUBS,)),
            dma((nz, SUBS)),
            dma((nz, SUBS)),
            dma((nz, SUBS)),
            dma((npool,)),
            dma((npool,)),
            dma((npool,)),
            dma((npool,)),
            dma((npool,)),
            dma((npool,)),
            dma((npool,)),
            dma((2, SUBS)),
            dma((SUBS,)),
            dma((SUBS,)),
        ],
        compiler_params=pltpu.CompilerParams(
            collective_id=0, has_side_effects=True, vmem_limit_bytes=54 * 1024 * 1024
        ),
    )(tokens, base_w, down_w, up_w, ids, counts, row_table)


def solution(mesh):
    in_specs = (
        P(("group", "pool"), "tensor"),
        P("tensor", None),
        P(("group", "pool"), "tensor", None),
        P(("group", "pool"), None, "tensor"),
        P(("group", "pool"), None),
        P(("group", "pool"), None),
        P("group"),
    )
    out_specs = P(("group", "pool"), "tensor")
    return jax.shard_map(body, mesh=mesh, in_specs=in_specs, out_specs=out_specs, check_vma=False)
```

```python
import functools

import jax
import jax.numpy as jnp
from jax import lax
from jax.experimental import pallas as pl
from jax.experimental.pallas import tpu as pltpu
from jax.sharding import PartitionSpec as P

DRAFT = 8
CAP = 2
SUBS = 4
HELD = 2
MESH = pl.DeviceIdType.MESH
F32 = jnp.float32
BF16 = jnp.bfloat16


def kernel(
    nz,
    npool,
    tok_hbm,
    w_hbm,
    down_hbm,
    up_hbm,
    ids,
    counts,
    row_table,
    out_hbm,
    tok,
    w,
    down,
    up,
    part,
    right_in,
    left_in,
    down_send,
    down_got,
    up_send,
    up_got,
    shrink,
    shr_pack,
    shr_in,
    mixed,
    out_v,
    req_out,
    req_in,
    req_s,
    own_s,
    span_s,
    batch_s,
    tok_sem,
    w_sem,
    down_sem,
    up_sem,
    out_sem,
    part_send,
    right_recv,
    left_recv,
    req_send,
    req_recv,
    req_local,
    down_send_sem,
    down_recv,
    up_send_sem,
    up_recv,
    shr_send_sem,
    shr_recv,
):
    z = lax.axis_index("tensor")
    me = lax.axis_index("pool")
    slots = down_hbm.shape[0]
    batches = ids.shape[1]
    sub = tok.shape[1]
    cw = out_v.shape[2]
    rank2 = down_hbm.shape[2]
    rank = rank2 // 2
    first, last = z == 0, z == nz - 1
    middle = jnp.logical_and(z > 0, z < nz - 1)
    upper = lax.div(2 * z, nz)

    def chunk(i):
        return i + (1 - upper) * (nz - 1 - 2 * i)

    def peer(j):
        return lax.rem(lax.div(me, 2) + lax.div(j, 2), npool // 2) * 2 + lax.rem(me + j, 2)

    def tok_copy(s):
        return pltpu.make_async_copy(tok_hbm.at[pl.ds(s * sub, sub)], tok.at[s], tok_sem.at[s])

    def w_copy(d):
        return pltpu.make_async_copy(
            w_hbm.at[:, pl.ds(pl.multiple_of(d * cw, cw), cw)], w.at[d], w_sem.at[d]
        )

    down_copy = pltpu.make_async_copy(down_hbm, down, down_sem)
    up_copy = pltpu.make_async_copy(up_hbm, up, up_sem)

    def right_copy(d, s):
        return pltpu.make_async_remote_copy(
            src_ref=part.at[d, s],
            dst_ref=right_in.at[d, s],
            send_sem=part_send.at[d, s],
            recv_sem=right_recv.at[d, s],
            device_id={"tensor": z + 1},
            device_id_type=MESH,
        )

    def left_copy(d, s):
        return pltpu.make_async_remote_copy(
            src_ref=part.at[d, s],
            dst_ref=left_in.at[d, s],
            send_sem=part_send.at[d, s],
            recv_sem=left_recv.at[d, s],
            device_id={"tensor": z - 1},
            device_id_type=MESH,
        )

    def shr_copy(to, landing):
        return pltpu.make_async_remote_copy(
            src_ref=shr_pack.at[lax.div(2 * to, nz)],
            dst_ref=shr_in.at[landing],
            send_sem=shr_send_sem.at[to],
            recv_sem=shr_recv.at[landing],
            device_id={"tensor": to},
            device_id_type=MESH,
        )

    def pool_copy(src, dst, send, recv, p, landing):
        return pltpu.make_async_remote_copy(
            src_ref=src,
            dst_ref=dst,
            send_sem=send.at[p],
            recv_sem=recv.at[landing],
            device_id={"pool": p},
            device_id_type=MESH,
        )

    def req_copy(p, landing):
        return pool_copy(req_out.at[p], req_in.at[landing], req_send, req_recv, p, landing)

    def down_peer(p, landing):
        return pool_copy(
            down_send.at[p], down_got.at[landing], down_send_sem, down_recv, p, landing
        )

    def up_rows(p):
        return pl.ds(pl.multiple_of(p * rank2, rank2), rank2)

    def up_peer(p, landing):
        return pool_copy(
            up_send.at[p], up_got.at[up_rows(landing)], up_send_sem, up_recv, p, landing
        )

    w_copy(chunk(0)).start()
    for s in range(SUBS):
        tok_copy(s).start()
    down_copy.start()
    up_copy.start()
    for i in range(1, nz):
        w_copy(chunk(i)).start()

    barrier = pltpu.get_barrier_semaphore()

    def line_peer(j):
        return lax.rem(z + j, nz)

    for j in range(1, nz):
        pl.semaphore_signal(
            barrier, inc=1, device_id={"tensor": line_peer(j)}, device_id_type=MESH
        )

    for j in range(1, npool):
        p = peer(jnp.int32(j))
        pl.semaphore_signal(barrier, inc=1, device_id={"pool": p}, device_id_type=MESH)

    def read_batch(b, row):
        index = row_table[ids[0, b]]
        batch_s[0, b] = index // slots
        batch_s[1, b] = lax.rem(index, slots)
        batch_s[2, b] = row
        after = row + counts[0, b] * DRAFT
        batch_s[3, b] = after
        return after

    lax.fori_loop(0, batches, read_batch, jnp.int32(0))
    lane8 = lax.broadcasted_iota(jnp.int32, (8, 128), 1)

    def read_holder(p, _):
        def match(b, carry):
            seen, r0, b0, e0, r1, b1, e1 = carry
            hit = batch_s[0, b] == p
            one = jnp.logical_and(hit, seen == 0)
            two = jnp.logical_and(hit, seen == 1)
            local, start, end = batch_s[1, b], batch_s[2, b], batch_s[3, b]
            return (
                seen + jnp.where(hit, 1, 0),
                jnp.where(one, local, r0),
                jnp.where(one, start, b0),
                jnp.where(one, end, e0),
                jnp.where(two, local, r1),
                jnp.where(two, start, b1),
                jnp.where(two, end, e1),
            )

        zero = jnp.int32(0)
        _, r0, b0, e0, r1, b1, e1 = lax.fori_loop(0, batches, match, (zero,) * 7)
        own_s[p, 0] = r0
        own_s[p, 1] = r1
        span_s[p, 0] = b0
        span_s[p, 1] = e0
        span_s[p, 2] = b1
        span_s[p, 3] = e1
        req_out[p] = jnp.where(lane8 == 0, r0, jnp.where(lane8 == 1, r1, 0))
        return 0

    lax.fori_loop(0, npool, read_holder, 0)
    pl.semaphore_wait(barrier, npool - 1 + nz - 1)

    def each_peer(body):
        def step(j, _):
            body(peer(j))
            return 0

        lax.fori_loop(1, npool, step, 0)

    each_peer(lambda p: req_copy(p, me).start())

    def base_block(d, s):
        part[d, s] = jnp.dot(tok[s], w[d], preferred_element_type=F32).astype(BF16)

    def end_send(d, s):
        @pl.when(first)
        def _():
            right_copy(d, s).start()

        @pl.when(last)
        def _():
            left_copy(d, s).start()

    w_copy(chunk(0)).wait()

    def first_chunk(s, _):
        tok_copy(s).wait()
        base_block(chunk(0), s)
        end_send(chunk(0), s)
        return 0

    lax.fori_loop(0, SUBS, first_chunk, 0)

    down_copy.wait()
    up_copy.wait()
    for c in range(CAP):
        down_got[me, :, c * rank2 : (c + 1) * rank2] = down[own_s[me, c]]
        up_got[pl.ds(pl.multiple_of(me * rank2 + c * rank, rank), rank), :] = up[own_s[me, c]]

    def read_request(p):
        req_copy(p, p).wait_recv()
        local = pltpu.make_async_copy(req_in.at[p], req_s.at[p], req_local.at[p])
        local.start()
        local.wait()

    each_peer(read_request)

    def serve(p):
        for c in range(CAP):
            down_send[p, :, c * rank2 : (c + 1) * rank2] = down[req_s[p, 0, c]]
            up_send[p, c * rank : (c + 1) * rank, :] = up[req_s[p, 0, c]]
        down_peer(p, me).start()
        up_peer(p, me).start()

    each_peer(serve)

    def next_chunk(i, _):
        d = chunk(i)
        w_copy(d).wait()

        def rows(s, _):
            base_block(d, s)

            @pl.when(jnp.logical_or(i < nz - 2, jnp.logical_and(i == nz - 2, s < SUBS - HELD)))
            def _():
                end_send(d, s)

            return 0

        return lax.fori_loop(0, SUBS, rows, 0)

    lax.fori_loop(1, nz, next_chunk, 0)

    shrink[...] = jnp.zeros_like(shrink)
    row_of = lax.broadcasted_iota(jnp.int32, (sub, rank2), 0)

    def down_project(p):
        def rows(s, _):
            both = jnp.dot(tok[s], down_got[p], preferred_element_type=F32)
            at = row_of + s * sub
            kept = shrink[s]
            for c in range(CAP):
                use = jnp.logical_and(at >= span_s[p, 2 * c], at < span_s[p, 2 * c + 1])
                kept = jnp.where(use, both[:, c * rank2 : (c + 1) * rank2], kept)
            shrink[s] = kept
            return 0

        lax.fori_loop(0, SUBS, rows, 0)

    def down_from(j, _):
        p = peer(j)
        down_peer(p, p).wait_recv()
        down_project(p)
        return 0

    down_project(me)
    lax.fori_loop(1, 2, down_from, 0)

    @pl.when(middle)
    def _():
        def forward(t, _):
            right_at, left_at = t - z, t - (nz - 1 - z)
            r, rs = nz - 1 - lax.div(right_at, SUBS), lax.rem(right_at, SUBS)
            l, ls = lax.div(left_at, SUBS), lax.rem(left_at, SUBS)

            @pl.when(jnp.logical_and(right_at >= 0, r > z))
            def _():
                right_copy(r, rs).wait_recv()
                part[r, rs] = (part[r, rs].astype(F32) + right_in[r, rs].astype(F32)).astype(BF16)
                right_copy(r, rs).start()

            @pl.when(jnp.logical_and(left_at >= 0, l < z))
            def _():
                left_copy(l, ls).wait_recv()
                part[l, ls] = (part[l, ls].astype(F32) + left_in[l, ls].astype(F32)).astype(BF16)
                left_copy(l, ls).start()

            return 0

        lax.fori_loop(0, (nz - 2) * SUBS + 1, forward, 0)

    lax.fori_loop(2, npool, down_from, 0)

    lane = lax.broadcasted_iota(jnp.int32, (sub, rank2), 1)

    def pack(s, _):
        a, b = shrink[s], shrink[s + SUBS // 2]
        shr_pack[0, s] = jnp.where(lane < rank, a, pltpu.roll(b, rank, 1)).astype(BF16)
        shr_pack[1, s] = jnp.where(lane < rank, pltpu.roll(a, rank, 1), b).astype(BF16)
        return 0

    lax.fori_loop(0, SUBS // 2, pack, 0)

    def each_line_peer(body):
        def step(j, _):
            body(line_peer(j))
            return 0

        lax.fori_loop(1, nz, step, 0)

    each_line_peer(lambda to: shr_copy(to, z).start())
    for s in range(SUBS - HELD, SUBS):
        end_send(chunk(nz - 2), s)

    each_peer(lambda p: up_peer(p, p).wait_recv())
    each_line_peer(lambda p: shr_copy(p, p).wait_recv())
    for s in range(SUBS // 2):
        shrink[s] = shr_pack[upper, s].astype(F32)

        def add(p, s=s):
            shrink[s] = shrink[s] + shr_in[p, s].astype(F32)

        each_line_peer(add)

    def finish(s, _):
        packed = shrink[lax.rem(s, SUBS // 2)]
        swapped = pltpu.roll(packed, rank, 1)
        half = jnp.where(lane // rank == lax.div(s, SUBS // 2), packed, swapped)
        at = row_of + s * sub
        for p in range(npool):
            begin = jnp.where(lane < rank, span_s[p, 0], span_s[p, 2])
            end = jnp.where(lane < rank, span_s[p, 1], span_s[p, 3])
            use = jnp.logical_and(at >= begin, at < end)
            mixed[:, p * rank2 : (p + 1) * rank2] = jnp.where(use, half, 0.0).astype(BF16)
        out = jnp.dot(mixed[...], up_got[...], preferred_element_type=F32)
        out_v[s] = out + part[z, s].astype(F32)

        @pl.when(z > 0)
        def _():
            right_copy(z, s).wait_recv()
            out_v[s] = out_v[s] + right_in[z, s].astype(F32)

        @pl.when(z < nz - 1)
        def _():
            left_copy(z, s).wait_recv()
            out_v[s] = out_v[s] + left_in[z, s].astype(F32)

        part[z, s] = out_v[s].astype(BF16)
        pltpu.make_async_copy(
            part.at[z, s], out_hbm.at[pl.ds(pl.multiple_of(s * sub, sub), sub)], out_sem.at[s]
        ).start()
        return 0

    lax.fori_loop(0, SUBS, finish, 0)

    def sent(s, _):
        pltpu.make_async_copy(
            part.at[z, s], out_hbm.at[pl.ds(pl.multiple_of(s * sub, sub), sub)], out_sem.at[s]
        ).wait()

        def one(d, _):
            @pl.when(d > z)
            def _():
                right_copy(d, s).wait_send()

            @pl.when(d < z)
            def _():
                left_copy(d, s).wait_send()

            return 0

        lax.fori_loop(0, nz, one, 0)

        return 0

    lax.fori_loop(0, SUBS, sent, 0)

    def pool_sent(p):
        req_copy(p, me).wait_send()
        down_peer(p, me).wait_send()
        up_peer(p, me).wait_send()

    each_peer(pool_sent)
    each_line_peer(lambda to: shr_copy(to, z).wait_send())


def body(tokens, base_w, down_w, up_w, ids, counts, row_table):
    nz, npool = lax.axis_size("tensor"), lax.axis_size("pool")
    rows, features = tokens.shape
    slots, _, rank2 = down_w.shape
    rank, cw = up_w.shape[1:]
    batches = ids.shape[1]
    sub = rows // SUBS
    any_spec = pl.BlockSpec(memory_space=pl.ANY)
    smem = pl.BlockSpec(memory_space=pltpu.SMEM)
    dma = pltpu.SemaphoreType.DMA
    vmem = pltpu.VMEM
    return pl.pallas_call(
        functools.partial(kernel, nz, npool),
        out_shape=jax.ShapeDtypeStruct((rows, cw), BF16),
        in_specs=[any_spec] * 4 + [smem] * 3,
        out_specs=any_spec,
        scratch_shapes=[
            vmem((SUBS, sub, features), BF16),
            vmem((nz, features, cw), BF16),
            vmem((slots, features, rank2), BF16),
            vmem((slots, rank, cw), BF16),
            vmem((nz, SUBS, sub, cw), BF16),
            vmem((nz, SUBS, sub, cw), BF16),
            vmem((nz, SUBS, sub, cw), BF16),
            vmem((npool, features, CAP * rank2), BF16),
            vmem((npool, features, CAP * rank2), BF16),
            vmem((npool, CAP * rank, cw), BF16),
            vmem((npool * CAP * rank, cw), BF16),
            vmem((SUBS, sub, rank2), F32),
            vmem((2, SUBS // 2, sub, rank2), BF16),
            vmem((nz, SUBS // 2, sub, rank2), BF16),
            vmem((sub, npool * CAP * rank), BF16),
            vmem((SUBS, sub, cw), F32),
            vmem((npool, 8, 128), jnp.int32),
            vmem((npool, 8, 128), jnp.int32),
            pltpu.SMEM((npool, 8, 128), jnp.int32),
            pltpu.SMEM((npool, CAP), jnp.int32),
            pltpu.SMEM((npool, 2 * CAP), jnp.int32),
            pltpu.SMEM((4, batches), jnp.int32),
            dma((SUBS,)),
            dma((nz,)),
            dma,
            dma,
            dma((SUBS,)),
            dma((nz, SUBS)),
            dma((nz, SUBS)),
            dma((nz, SUBS)),
            dma((npool,)),
            dma((npool,)),
            dma((npool,)),
            dma((npool,)),
            dma((npool,)),
            dma((npool,)),
            dma((npool,)),
            dma((nz,)),
            dma((nz,)),
        ],
        compiler_params=pltpu.CompilerParams(
            collective_id=0, has_side_effects=True, vmem_limit_bytes=54 * 1024 * 1024
        ),
    )(tokens, base_w, down_w, up_w, ids, counts, row_table)


def solution(mesh):
    in_specs = (
        P(("group", "pool"), "tensor"),
        P("tensor", None),
        P(("group", "pool"), "tensor", None),
        P(("group", "pool"), None, "tensor"),
        P(("group", "pool"), None),
        P(("group", "pool"), None),
        P("group"),
    )
    out_specs = P(("group", "pool"), "tensor")
    return jax.shard_map(body, mesh=mesh, in_specs=in_specs, out_specs=out_specs, check_vma=False)
```

```python
import functools

import jax
import jax.numpy as jnp
from jax import lax
from jax.experimental import pallas as pl
from jax.experimental.pallas import tpu as pltpu
from jax.sharding import PartitionSpec as P

DRAFT = 8
CAP = 2
SUBS = 2
HELD = 1
MESH = pl.DeviceIdType.MESH
F32 = jnp.float32
BF16 = jnp.bfloat16


def kernel(
    nz,
    npool,
    tok_hbm,
    w_hbm,
    down_hbm,
    up_hbm,
    ids,
    counts,
    row_table,
    out_hbm,
    tok,
    w,
    down,
    up,
    part,
    right_in,
    left_in,
    down_send,
    down_got,
    up_send,
    up_got,
    shrink,
    shr_pack,
    shr_in,
    mixed,
    out_v,
    req_out,
    req_in,
    req_s,
    own_s,
    span_s,
    batch_s,
    tok_sem,
    w_sem,
    down_sem,
    up_sem,
    out_sem,
    part_send,
    right_recv,
    left_recv,
    req_send,
    req_recv,
    req_local,
    down_send_sem,
    down_recv,
    up_send_sem,
    up_recv,
    shr_send_sem,
    shr_recv,
):
    z = lax.axis_index("tensor")
    me = lax.axis_index("pool")
    slots = down_hbm.shape[0]
    batches = ids.shape[1]
    sub = tok.shape[1]
    cw = out_v.shape[2]
    rank2 = down_hbm.shape[2]
    rank = rank2 // 2
    first, last = z == 0, z == nz - 1
    middle = jnp.logical_and(z > 0, z < nz - 1)
    upper = lax.div(2 * z, nz)

    def chunk(i):
        return i + (1 - upper) * (nz - 1 - 2 * i)

    def peer(j):
        return lax.rem(lax.div(me, 2) + lax.div(j, 2), npool // 2) * 2 + lax.rem(me + j, 2)

    def tok_copy(s):
        return pltpu.make_async_copy(tok_hbm.at[pl.ds(s * sub, sub)], tok.at[s], tok_sem.at[s])

    def w_copy(d):
        return pltpu.make_async_copy(
            w_hbm.at[:, pl.ds(pl.multiple_of(d * cw, cw), cw)], w.at[d], w_sem.at[d]
        )

    down_copy = pltpu.make_async_copy(down_hbm, down, down_sem)
    up_copy = pltpu.make_async_copy(up_hbm, up, up_sem)

    def right_copy(d, s):
        return pltpu.make_async_remote_copy(
            src_ref=part.at[d, s],
            dst_ref=right_in.at[d, s],
            send_sem=part_send.at[d, s],
            recv_sem=right_recv.at[d, s],
            device_id={"tensor": z + 1},
            device_id_type=MESH,
        )

    def left_copy(d, s):
        return pltpu.make_async_remote_copy(
            src_ref=part.at[d, s],
            dst_ref=left_in.at[d, s],
            send_sem=part_send.at[d, s],
            recv_sem=left_recv.at[d, s],
            device_id={"tensor": z - 1},
            device_id_type=MESH,
        )

    def shr_copy(to, landing):
        return pltpu.make_async_remote_copy(
            src_ref=shr_pack.at[lax.div(2 * to, nz)],
            dst_ref=shr_in.at[landing],
            send_sem=shr_send_sem.at[to],
            recv_sem=shr_recv.at[landing],
            device_id={"tensor": to},
            device_id_type=MESH,
        )

    def pool_copy(src, dst, send, recv, p, landing):
        return pltpu.make_async_remote_copy(
            src_ref=src,
            dst_ref=dst,
            send_sem=send.at[p],
            recv_sem=recv.at[landing],
            device_id={"pool": p},
            device_id_type=MESH,
        )

    def req_copy(p, landing):
        return pool_copy(req_out.at[p], req_in.at[landing], req_send, req_recv, p, landing)

    def down_peer(p, landing):
        return pool_copy(
            down_send.at[p], down_got.at[landing], down_send_sem, down_recv, p, landing
        )

    def up_rows(p):
        return pl.ds(pl.multiple_of(p * rank2, rank2), rank2)

    def up_peer(p, landing):
        return pool_copy(
            up_send.at[p], up_got.at[up_rows(landing)], up_send_sem, up_recv, p, landing
        )

    w_copy(chunk(0)).start()
    for s in range(SUBS):
        tok_copy(s).start()
    down_copy.start()
    up_copy.start()
    for i in range(1, nz):
        w_copy(chunk(i)).start()

    barrier = pltpu.get_barrier_semaphore()

    def line_peer(j):
        return lax.rem(z + j, nz)

    for j in range(1, nz):
        pl.semaphore_signal(
            barrier, inc=1, device_id={"tensor": line_peer(j)}, device_id_type=MESH
        )

    for j in range(1, npool):
        p = peer(jnp.int32(j))
        pl.semaphore_signal(barrier, inc=1, device_id={"pool": p}, device_id_type=MESH)

    def read_batch(b, row):
        index = row_table[ids[0, b]]
        batch_s[0, b] = index // slots
        batch_s[1, b] = lax.rem(index, slots)
        batch_s[2, b] = row
        after = row + counts[0, b] * DRAFT
        batch_s[3, b] = after
        return after

    lax.fori_loop(0, batches, read_batch, jnp.int32(0))
    lane8 = lax.broadcasted_iota(jnp.int32, (8, 128), 1)

    def read_holder(p, _):
        def match(b, carry):
            seen, r0, b0, e0, r1, b1, e1 = carry
            hit = batch_s[0, b] == p
            one = jnp.logical_and(hit, seen == 0)
            two = jnp.logical_and(hit, seen == 1)
            local, start, end = batch_s[1, b], batch_s[2, b], batch_s[3, b]
            return (
                seen + jnp.where(hit, 1, 0),
                jnp.where(one, local, r0),
                jnp.where(one, start, b0),
                jnp.where(one, end, e0),
                jnp.where(two, local, r1),
                jnp.where(two, start, b1),
                jnp.where(two, end, e1),
            )

        zero = jnp.int32(0)
        _, r0, b0, e0, r1, b1, e1 = lax.fori_loop(0, batches, match, (zero,) * 7)
        own_s[p, 0] = r0
        own_s[p, 1] = r1
        span_s[p, 0] = b0
        span_s[p, 1] = e0
        span_s[p, 2] = b1
        span_s[p, 3] = e1
        req_out[p] = jnp.where(lane8 == 0, r0, jnp.where(lane8 == 1, r1, 0))
        return 0

    lax.fori_loop(0, npool, read_holder, 0)
    pl.semaphore_wait(barrier, npool - 1 + nz - 1)

    def each_peer(body):
        def step(j, _):
            body(peer(j))
            return 0

        lax.fori_loop(1, npool, step, 0)

    each_peer(lambda p: req_copy(p, me).start())

    def base_block(d, s):
        part[d, s] = jnp.dot(tok[s], w[d], preferred_element_type=F32).astype(BF16)

    def end_send(d, s):
        @pl.when(first)
        def _():
            right_copy(d, s).start()

        @pl.when(last)
        def _():
            left_copy(d, s).start()

    w_copy(chunk(0)).wait()

    def first_chunk(s, _):
        tok_copy(s).wait()
        base_block(chunk(0), s)
        end_send(chunk(0), s)
        return 0

    lax.fori_loop(0, SUBS, first_chunk, 0)

    down_copy.wait()
    up_copy.wait()
    for c in range(CAP):
        down_got[me, :, c * rank2 : (c + 1) * rank2] = down[own_s[me, c]]
        up_got[pl.ds(pl.multiple_of(me * rank2 + c * rank, rank), rank), :] = up[own_s[me, c]]

    def read_request(p):
        req_copy(p, p).wait_recv()
        local = pltpu.make_async_copy(req_in.at[p], req_s.at[p], req_local.at[p])
        local.start()
        local.wait()

    each_peer(read_request)

    def serve(p):
        for c in range(CAP):
            down_send[p, :, c * rank2 : (c + 1) * rank2] = down[req_s[p, 0, c]]
            up_send[p, c * rank : (c + 1) * rank, :] = up[req_s[p, 0, c]]
        down_peer(p, me).start()
        up_peer(p, me).start()

    each_peer(serve)

    def next_chunk(i, _):
        d = chunk(i)
        w_copy(d).wait()

        def rows(s, _):
            base_block(d, s)

            @pl.when(jnp.logical_or(i < nz - 2, jnp.logical_and(i == nz - 2, s < SUBS - HELD)))
            def _():
                end_send(d, s)

            return 0

        return lax.fori_loop(0, SUBS, rows, 0)

    lax.fori_loop(1, nz, next_chunk, 0)

    shrink[...] = jnp.zeros_like(shrink)
    row_of = lax.broadcasted_iota(jnp.int32, (sub, rank2), 0)

    def down_project(p):
        def rows(s, _):
            both = jnp.dot(tok[s], down_got[p], preferred_element_type=F32)
            at = row_of + s * sub
            kept = shrink[s]
            for c in range(CAP):
                use = jnp.logical_and(at >= span_s[p, 2 * c], at < span_s[p, 2 * c + 1])
                kept = jnp.where(use, both[:, c * rank2 : (c + 1) * rank2], kept)
            shrink[s] = kept
            return 0

        lax.fori_loop(0, SUBS, rows, 0)

    def down_from(j, _):
        p = peer(j)
        down_peer(p, p).wait_recv()
        down_project(p)
        return 0

    down_project(me)
    lax.fori_loop(1, 2, down_from, 0)

    @pl.when(middle)
    def _():
        def forward(t, _):
            right_at, left_at = t - z, t - (nz - 1 - z)
            r, rs = nz - 1 - lax.div(right_at, SUBS), lax.rem(right_at, SUBS)
            l, ls = lax.div(left_at, SUBS), lax.rem(left_at, SUBS)

            @pl.when(jnp.logical_and(right_at >= 0, r > z))
            def _():
                right_copy(r, rs).wait_recv()
                part[r, rs] = (part[r, rs].astype(F32) + right_in[r, rs].astype(F32)).astype(BF16)
                right_copy(r, rs).start()

            @pl.when(jnp.logical_and(left_at >= 0, l < z))
            def _():
                left_copy(l, ls).wait_recv()
                part[l, ls] = (part[l, ls].astype(F32) + left_in[l, ls].astype(F32)).astype(BF16)
                left_copy(l, ls).start()

            return 0

        lax.fori_loop(0, (nz - 2) * SUBS + 1, forward, 0)

    lax.fori_loop(2, npool, down_from, 0)

    lane = lax.broadcasted_iota(jnp.int32, (sub, rank2), 1)

    def pack(s, _):
        a, b = shrink[s], shrink[s + SUBS // 2]
        shr_pack[0, s] = jnp.where(lane < rank, a, pltpu.roll(b, rank, 1)).astype(BF16)
        shr_pack[1, s] = jnp.where(lane < rank, pltpu.roll(a, rank, 1), b).astype(BF16)
        return 0

    lax.fori_loop(0, SUBS // 2, pack, 0)

    def each_line_peer(body):
        def step(j, _):
            body(line_peer(j + (1 - upper) * (nz - 2 * j)))
            return 0

        lax.fori_loop(1, nz, step, 0)

    each_line_peer(lambda to: shr_copy(to, z).start())
    for s in range(SUBS - HELD, SUBS):
        end_send(chunk(nz - 2), s)

    each_peer(lambda p: up_peer(p, p).wait_recv())
    each_line_peer(lambda p: shr_copy(p, p).wait_recv())
    for s in range(SUBS // 2):
        shrink[s] = shr_pack[upper, s].astype(F32)

        def add(p, s=s):
            shrink[s] = shrink[s] + shr_in[p, s].astype(F32)

        each_line_peer(add)

    def finish(s, _):
        packed = shrink[lax.rem(s, SUBS // 2)]
        swapped = pltpu.roll(packed, rank, 1)
        half = jnp.where(lane // rank == lax.div(s, SUBS // 2), packed, swapped)
        at = row_of + s * sub
        for p in range(npool):
            begin = jnp.where(lane < rank, span_s[p, 0], span_s[p, 2])
            end = jnp.where(lane < rank, span_s[p, 1], span_s[p, 3])
            use = jnp.logical_and(at >= begin, at < end)
            mixed[:, p * rank2 : (p + 1) * rank2] = jnp.where(use, half, 0.0).astype(BF16)
        out = jnp.dot(mixed[...], up_got[...], preferred_element_type=F32)
        out_v[s] = out + part[z, s].astype(F32)

        @pl.when(z > 0)
        def _():
            right_copy(z, s).wait_recv()
            out_v[s] = out_v[s] + right_in[z, s].astype(F32)

        @pl.when(z < nz - 1)
        def _():
            left_copy(z, s).wait_recv()
            out_v[s] = out_v[s] + left_in[z, s].astype(F32)

        part[z, s] = out_v[s].astype(BF16)
        pltpu.make_async_copy(
            part.at[z, s], out_hbm.at[pl.ds(pl.multiple_of(s * sub, sub), sub)], out_sem.at[s]
        ).start()
        return 0

    lax.fori_loop(0, SUBS, finish, 0)

    def sent(s, _):
        pltpu.make_async_copy(
            part.at[z, s], out_hbm.at[pl.ds(pl.multiple_of(s * sub, sub), sub)], out_sem.at[s]
        ).wait()

        def one(d, _):
            @pl.when(d > z)
            def _():
                right_copy(d, s).wait_send()

            @pl.when(d < z)
            def _():
                left_copy(d, s).wait_send()

            return 0

        lax.fori_loop(0, nz, one, 0)

        return 0

    lax.fori_loop(0, SUBS, sent, 0)

    def pool_sent(p):
        req_copy(p, me).wait_send()
        down_peer(p, me).wait_send()
        up_peer(p, me).wait_send()

    each_peer(pool_sent)
    each_line_peer(lambda to: shr_copy(to, z).wait_send())


def body(tokens, base_w, down_w, up_w, ids, counts, row_table):
    nz, npool = lax.axis_size("tensor"), lax.axis_size("pool")
    rows, features = tokens.shape
    slots, _, rank2 = down_w.shape
    rank, cw = up_w.shape[1:]
    batches = ids.shape[1]
    sub = rows // SUBS
    any_spec = pl.BlockSpec(memory_space=pl.ANY)
    smem = pl.BlockSpec(memory_space=pltpu.SMEM)
    dma = pltpu.SemaphoreType.DMA
    vmem = pltpu.VMEM
    return pl.pallas_call(
        functools.partial(kernel, nz, npool),
        out_shape=jax.ShapeDtypeStruct((rows, cw), BF16),
        in_specs=[any_spec] * 4 + [smem] * 3,
        out_specs=any_spec,
        scratch_shapes=[
            vmem((SUBS, sub, features), BF16),
            vmem((nz, features, cw), BF16),
            vmem((slots, features, rank2), BF16),
            vmem((slots, rank, cw), BF16),
            vmem((nz, SUBS, sub, cw), BF16),
            vmem((nz, SUBS, sub, cw), BF16),
            vmem((nz, SUBS, sub, cw), BF16),
            vmem((npool, features, CAP * rank2), BF16),
            vmem((npool, features, CAP * rank2), BF16),
            vmem((npool, CAP * rank, cw), BF16),
            vmem((npool * CAP * rank, cw), BF16),
            vmem((SUBS, sub, rank2), F32),
            vmem((2, SUBS // 2, sub, rank2), BF16),
            vmem((nz, SUBS // 2, sub, rank2), BF16),
            vmem((sub, npool * CAP * rank), BF16),
            vmem((SUBS, sub, cw), F32),
            vmem((npool, 8, 128), jnp.int32),
            vmem((npool, 8, 128), jnp.int32),
            pltpu.SMEM((npool, 8, 128), jnp.int32),
            pltpu.SMEM((npool, CAP), jnp.int32),
            pltpu.SMEM((npool, 2 * CAP), jnp.int32),
            pltpu.SMEM((4, batches), jnp.int32),
            dma((SUBS,)),
            dma((nz,)),
            dma,
            dma,
            dma((SUBS,)),
            dma((nz, SUBS)),
            dma((nz, SUBS)),
            dma((nz, SUBS)),
            dma((npool,)),
            dma((npool,)),
            dma((npool,)),
            dma((npool,)),
            dma((npool,)),
            dma((npool,)),
            dma((npool,)),
            dma((nz,)),
            dma((nz,)),
        ],
        compiler_params=pltpu.CompilerParams(
            collective_id=0, has_side_effects=True, vmem_limit_bytes=54 * 1024 * 1024
        ),
    )(tokens, base_w, down_w, up_w, ids, counts, row_table)


def solution(mesh):
    in_specs = (
        P(("group", "pool"), "tensor"),
        P("tensor", None),
        P(("group", "pool"), "tensor", None),
        P(("group", "pool"), None, "tensor"),
        P(("group", "pool"), None),
        P(("group", "pool"), None),
        P("group"),
    )
    out_specs = P(("group", "pool"), "tensor")
    return jax.shard_map(body, mesh=mesh, in_specs=in_specs, out_specs=out_specs, check_vma=False)
```
